256 devices in a mesh: grp: 8 (over z_hi, core), ep: 32 (over x, z_lo, y).
Axes of the slice: x: 4, y: 4, z: 8 (z_hi: 4, z_lo: 2; z = z_hi * 2 + z_lo), core: 2. Of those that a mesh axis runs over, the one named last changes fastest.
Arguments:
- out_grad: bfloat16 [131072, 2048], P(('grp', 'ep')), may hold values from -0.5 to 0.5
- probs: float32 [131072, 8], P(('grp', 'ep')), may hold values from 0.02 to 0.5
- dest: int32 [131072, 8], P(('grp', 'ep')), may hold values from -1 to 98303, as said below
- replica_owner: int32 [8, 32], P('grp'), may hold values from 0 to 31, as said below
- gate_up: bfloat16 [786432, 1536], P(('grp', 'ep')), may hold values from -6 to 6
Outputs:
- d_down: float32 [32, 768, 2048], P('ep', None, 'grp')
The draws below stay inside these ranges and needn't reach their ends.
Inputs may be any that keep to these rules, and one draw needn't show every extreme that they name: `dest`: copies of one token name distinct rows; a device's copies to slot buffer (j, s) fill the rows of that buffer's block for the device, which is the device's ep index times 48 onward, from its start without gaps; in every draw some device fills its block of some buffer, all 48 rows, and copies beyond a block are dropped. `replica_owner`: each entry names an expert that has its primary slot on that ep index of the group.
All inputs are finite; a program needn't handle non-finite values.
Results may differ from the reference program's by a relative error of at most 0.005.
Values may be sent and summed in bfloat16 or wider, within the bound.
No kernel may reach another device: no remote copies, remote signals or barrier semaphores. Data moves between devices by JAX's collectives and lax.ppermute only.
A program may use at most 128 MiB of HBM per device.

```python
import math
import jax
import jax.numpy as jnp
from jax import lax

D = 2048
H = 768
TOP = 8
TOK_DEV = 512
EXPERTS = 32
HOT = 8
CAP = 1536
C_SRC = 48
TOKEN_TOTAL = 131072
SLOT_ROWS = 786432
N_GRP = 8
N_EP = 32


def plan_group(group_key):
    first, second_replica, third = jax.random.split(group_key, 3)
    experts = jnp.arange(EXPERTS, dtype=jnp.int32)
    order = jax.random.permutation(first, EXPERTS).astype(jnp.int32)
    hotness = jnp.zeros((EXPERTS,), jnp.int32).at[order[:HOT]].set(1)
    owners = order[jax.random.randint(second_replica, (EXPERTS,), 0, HOT)]
    bits = jax.random.randint(third, (EXPERTS * TOK_DEV, EXPERTS), 0, 1 << 20)
    score = bits * (1 + 2 * hotness)[None, :] * 64 + experts[None, :]
    unused, chosen_experts = lax.top_k(score, TOP)
    chosen_experts = chosen_experts.astype(jnp.int32).reshape(EXPERTS, TOK_DEV * TOP)
    onehot = (chosen_experts[:, :, None] == experts[None, None, :]).astype(jnp.int32)
    before = jnp.cumsum(onehot, axis=1) - onehot
    count = jnp.sum(before * onehot, axis=2)
    match_flags = (owners[None, :] == experts[:, None]).astype(jnp.int32)
    slot_count = 1 + jnp.sum(match_flags, axis=1)
    ranks = jnp.cumsum(match_flags, axis=1) * match_flags
    token_share = slot_count[chosen_experts]
    turn = count % token_share
    place = count // token_share
    picked = jnp.sum(experts[None, None, :] * (ranks[chosen_experts] == turn[:, :, None]).astype(jnp.int32), axis=2)
    device = jnp.where(turn == 0, chosen_experts, picked)
    second_slot = jnp.where(turn == 0, 0, 1)
    source = experts[:, None]
    target = device * 2 * CAP + second_slot * CAP + source * C_SRC + place
    target = jnp.where(place < C_SRC, target, -1)
    return (owners, target.reshape(EXPERTS * TOK_DEV, TOP))


def plan_all(key):
    base = jax.random.fold_in(key, 7)
    keys = jax.random.split(base, N_GRP)
    owners, targets = jax.vmap(plan_group)(keys)
    return (owners.astype(jnp.int32), targets.reshape(N_GRP * EXPERTS * TOK_DEV, TOP).astype(jnp.int32))


def draw_dest(key, part):
    owners, targets = plan_all(key)
    return targets


def draw_replica_owner(key, part):
    owners, targets = plan_all(key)
    return owners


def block_levels(stream_key, dims, pieces, low, top_value):
    def one(axis_at, shards_of):
        heights = jax.random.uniform(jax.random.fold_in(jax.random.fold_in(stream_key, 6), axis_at), (shards_of,), jnp.float32, low / len(pieces), top_value / len(pieces))
        return jnp.repeat(jnp.exp(heights), dims[axis_at] // shards_of).reshape((-1,) + (1,) * (len(dims) - axis_at - 1))

    level = one(*pieces[0])
    for cut in pieces[1:]:
        level = level * one(*cut)
    return level


def bell_draw(key, dims, spread, reach, cuts=(), kind=jnp.bfloat16):
    drawn = jax.random.normal(key, dims, jnp.float32) * spread
    if len(cuts) > 0:
        drawn = block_levels(key, dims, cuts, -0.22, 0.18) * drawn
    return jnp.clip(drawn, min=-reach, max=reach).astype(kind)


def setup_inputs(seed: int = 0) -> dict:
    arg_keys = jax.random.split(jax.random.key(seed), 6)
    out_grad = bell_draw(arg_keys[0], (TOKEN_TOTAL, D), 0.08, 0.5, ((0, 256),))
    probs = jnp.clip(jnp.exp(math.log(0.5) - 3.218876 * jax.random.uniform(arg_keys[1], (TOKEN_TOTAL, TOP), jnp.float32) ** block_levels(arg_keys[1], (TOKEN_TOTAL, TOP), ((0, 256),), -0.2, 0.2)), 0.02, 0.5)
    dest = draw_dest(jax.random.fold_in(arg_keys[5], 71), 0)
    replica_owner = draw_replica_owner(jax.random.fold_in(arg_keys[5], 71), 0)
    gate_up = bell_draw(arg_keys[4], (SLOT_ROWS, 2 * H), 1.0, 6.0, ((0, 256),))
    return {"out_grad": out_grad, "probs": probs, "dest": dest, "replica_owner": replica_owner, "gate_up": gate_up}


def reference(out_grad, probs, dest, replica_owner, gate_up):
    group_rows = 2 * N_EP * CAP
    group_tokens = N_EP * TOK_DEV
    total = jnp.zeros((N_EP, H, D), jnp.float32)
    for group in range(N_GRP):
        lower = group * group_tokens
        grad_rows = out_grad[lower:lower + group_tokens]
        flat_weights = probs[lower:lower + group_tokens].astype(jnp.float32).reshape(-1)
        targets = dest[lower:lower + group_tokens].astype(jnp.int32)
        index = jnp.where(targets >= 0, targets, group_rows).reshape(-1).astype(jnp.int32)
        copy_of = jnp.full((group_rows,), -1, jnp.int32).at[index].set(
            jnp.arange(group_tokens * TOP, dtype=jnp.int32), mode="drop")
        owners = replica_owner[group].astype(jnp.int32)
        row_start = group * group_rows

        def per_device(device, carry):
            device = jnp.asarray(device).astype(jnp.int32)
            base = (device * 2 * CAP).astype(jnp.int32)
            rows = lax.dynamic_slice_in_dim(copy_of, base, 2 * CAP, 0)
            safe = jnp.maximum(rows, 0).astype(jnp.int32)
            weight = jnp.where(rows >= 0, flat_weights[safe], jnp.zeros_like(flat_weights[safe]))
            picked = grad_rows[(safe // TOP).astype(jnp.int32)].astype(jnp.float32)
            grads = (weight[:, None] * picked).astype(jnp.bfloat16)
            saved = lax.dynamic_slice_in_dim(gate_up, (base + row_start).astype(jnp.int32), 2 * CAP, 0)
            act = (jax.nn.silu(saved[:, :H].astype(jnp.float32)) * saved[:, H:].astype(jnp.float32)).astype(jnp.bfloat16)
            tile_main = jnp.dot(act[:CAP].T, grads[:CAP], preferred_element_type=jnp.float32).astype(jnp.bfloat16)
            tile_copy = jnp.dot(act[CAP:].T, grads[CAP:], preferred_element_type=jnp.float32).astype(jnp.bfloat16)
            tile_main, tile_copy = lax.optimization_barrier((tile_main, tile_copy))
            carry = carry.at[device].add(tile_main.astype(jnp.float32))
            carry = carry.at[owners[device]].add(tile_copy.astype(jnp.float32))
            return carry

        total = lax.fori_loop(0, N_EP, per_device, total)
    return total
```

```python
import functools

import jax
import jax.numpy as jnp
from jax import lax
from jax.experimental import pallas as pl
from jax.experimental.pallas import tpu as pltpu
from jax.sharding import PartitionSpec as P

VMEM_LIMIT = 56 * 1024 * 1024


def dispatch_kernel(per_src, rows_slot, block, dest_ref, probs_ref, grad_ref, first_ref, second_ref, target_ref):
    step = pl.program_id(0)

    @pl.when(step == 0)
    def _():
        dest = dest_ref[...]
        block_of = (jnp.maximum(dest, 0) // 16 * 21846) >> 16
        place = dest - block_of * per_src
        device_of = block_of >> 6
        second = (block_of >> 5) & 1
        target = second * rows_slot + device_of * per_src + place
        target_ref[...] = jnp.where(dest >= 0, target, -1)

    tokens = grad_ref.shape[0]
    rows = lax.broadcasted_iota(jnp.int32, (block, tokens), 0) + step * block
    weights = jnp.zeros((block, tokens), jnp.float32)
    for k in range(dest_ref.shape[0]):
        weights = jnp.where(target_ref[k : k + 1, :] == rows, probs_ref[k : k + 1, :], weights)
    pick = jnp.where(weights != 0.0, 1.0, 0.0).astype(jnp.bfloat16)
    weight = jnp.sum(weights, axis=1, keepdims=True)
    picked = jnp.dot(pick, grad_ref[...], preferred_element_type=jnp.float32)
    scaled = (weight * picked).astype(jnp.bfloat16)

    @pl.when(step < rows_slot // block)
    def _():
        first_ref[...] = scaled

    @pl.when(step >= rows_slot // block)
    def _():
        second_ref[...] = scaled


def dispatch(out_grad, probs, dest, n_ep, per_src):
    tokens, width = out_grad.shape
    top = probs.shape[1]
    rows_slot = n_ep * per_src
    block = 256
    per_slot = rows_slot // block
    return pl.pallas_call(
        functools.partial(dispatch_kernel, per_src, rows_slot, block),
        grid=(2 * per_slot,),
        in_specs=[
            pl.BlockSpec((top, tokens), lambda i: (0, 0)),
            pl.BlockSpec((top, tokens), lambda i: (0, 0)),
            pl.BlockSpec((tokens, width), lambda i: (0, 0)),
        ],
        out_specs=[
            pl.BlockSpec((block, width), lambda i: (jnp.minimum(i, per_slot - 1), 0)),
            pl.BlockSpec((block, width), lambda i: (jnp.maximum(i - per_slot, 0), 0)),
        ],
        out_shape=[jax.ShapeDtypeStruct((rows_slot, width), jnp.bfloat16)] * 2,
        scratch_shapes=[pltpu.VMEM((top, tokens), jnp.int32)],
        compiler_params=pltpu.CompilerParams(vmem_limit_bytes=VMEM_LIMIT),
    )(dest.T, probs.T, out_grad)


def tile_kernel(chunks, gate_up_ref, grads_ref, out_ref, act_ref):
    step = pl.program_id(0)
    rows, hidden2 = gate_up_ref.shape
    hidden = hidden2 // 2
    for c in range(chunks):

        @pl.when(step == c)
        def _():
            half = gate_up_ref[:, :hidden].astype(jnp.float32) * 0.5
            up = gate_up_ref[:, hidden:].astype(jnp.float32)
            act = ((half + half * jnp.tanh(half)) * up).astype(jnp.bfloat16)
            act_ref[:, c * rows : (c + 1) * rows] = act.T

    @pl.when(step >= chunks)
    def _():
        tile = jnp.dot(act_ref[...], grads_ref[...], preferred_element_type=jnp.float32)
        cols = out_ref.shape[2]
        for b in range(out_ref.shape[0]):
            out_ref[b] = tile[:, b * cols : (b + 1) * cols].astype(out_ref.dtype)


def slot_tile(gate_up, grads, slot, n_grp, dtype):
    cap, width = grads.shape
    hidden2 = gate_up.shape[1]
    hidden = hidden2 // 2
    chunks = 3
    rows = cap // chunks
    cols = width // n_grp
    per_step = 2
    steps = n_grp // per_step
    return pl.pallas_call(
        functools.partial(tile_kernel, chunks),
        grid=(chunks + steps,),
        in_specs=[
            pl.BlockSpec((rows, hidden2), lambda i: (slot * chunks + jnp.minimum(i, chunks - 1), 0)),
            pl.BlockSpec((cap, per_step * cols), lambda i: (0, jnp.maximum(i - chunks, 0))),
        ],
        out_specs=pl.BlockSpec((per_step, hidden, cols), lambda i: (jnp.maximum(i - chunks, 0), 0, 0)),
        out_shape=jax.ShapeDtypeStruct((n_grp, hidden, cols), dtype),
        scratch_shapes=[pltpu.VMEM((hidden, cap), jnp.bfloat16)],
        compiler_params=pltpu.CompilerParams(vmem_limit_bytes=VMEM_LIMIT),
    )(gate_up, grads)


def owner_sum_kernel(owners_ref, pieces_ref, out_ref, sum_ref):
    n_grp, n_ep = owners_ref.shape
    sum_ref[...] = jnp.zeros_like(sum_ref)

    def group(g, carry):
        def one(j, inner):
            owner = owners_ref[g, j]
            sum_ref[owner] += pieces_ref[g * n_ep + j].astype(jnp.float32)
            return inner

        return lax.fori_loop(0, n_ep, one, carry, unroll=8)

    lax.fori_loop(0, n_grp, group, 0)
    out_ref[...] = sum_ref[...].astype(out_ref.dtype)


def owner_sum(owners, pieces, n_ep):
    _, rows, cols = pieces.shape
    return pl.pallas_call(
        owner_sum_kernel,
        in_specs=[
            pl.BlockSpec(memory_space=pltpu.SMEM),
            pl.BlockSpec(memory_space=pltpu.VMEM),
        ],
        out_specs=pl.BlockSpec(memory_space=pltpu.VMEM),
        out_shape=jax.ShapeDtypeStruct((n_ep, rows, cols), jnp.bfloat16),
        scratch_shapes=[pltpu.VMEM((n_ep, rows, cols), jnp.float32)],
        compiler_params=pltpu.CompilerParams(vmem_limit_bytes=VMEM_LIMIT),
    )(owners, pieces)


def on_device(out_grad, probs, dest, replica_owner, gate_up):
    n_ep = lax.axis_size("ep")
    n_grp = lax.axis_size("grp")
    width = out_grad.shape[1]
    cap = gate_up.shape[0] // 2
    hidden = gate_up.shape[1] // 2
    per_src = cap // n_ep
    cols = width // n_grp
    rows = hidden // n_ep

    me = lax.axis_index("grp")
    owners = jnp.where(jnp.arange(n_grp, dtype=jnp.int32)[:, None] == me, replica_owner, 0)
    reach = 1
    while reach < n_grp:
        owners += lax.ppermute(owners, "grp", [(g, g ^ reach) for g in range(n_grp)])
        reach *= 2

    first, second = dispatch(out_grad, probs, dest, n_ep, per_src)

    def exchange(x):
        return lax.all_to_all(x, "ep", split_axis=0, concat_axis=0, tiled=True)

    main_rows = exchange(first.reshape(n_ep, per_src, width)).reshape(cap, width)
    main_tile = slot_tile(gate_up, main_rows, 0, n_grp, jnp.bfloat16)
    second, main_tile = lax.optimization_barrier((second, main_tile))
    main_sum = lax.psum_scatter(main_tile, "grp", scatter_dimension=0, tiled=True)
    copy_rows = exchange(second.reshape(n_ep, per_src, width)).reshape(cap, width)
    copy_tile = slot_tile(gate_up, copy_rows, 1, n_grp, jnp.bfloat16)
    copy_tile, main_sum = lax.optimization_barrier((copy_tile, main_sum))
    pieces = lax.all_to_all(
        copy_tile.reshape(n_grp * n_ep, rows, cols), ("grp", "ep"), split_axis=0, concat_axis=0, tiled=True
    )
    blocks = owner_sum(owners, pieces, n_ep)
    owned = exchange(blocks).reshape(1, hidden, cols)
    return main_sum.astype(jnp.float32) + owned.astype(jnp.float32)


def solution(mesh):
    in_specs = (
        P(("grp", "ep"), None),
        P(("grp", "ep"), None),
        P(("grp", "ep"), None),
        P("grp", None),
        P(("grp", "ep"), None),
    )
    out_specs = P("ep", None, "grp")
    return jax.shard_map(
        on_device, mesh=mesh, in_specs=in_specs, out_specs=out_specs, check_vma=False
    )
```

```python
import functools

import jax
import jax.numpy as jnp
from jax import lax
from jax.experimental import pallas as pl
from jax.experimental.pallas import tpu as pltpu
from jax.sharding import PartitionSpec as P

VMEM_LIMIT = 56 * 1024 * 1024


def dispatch_kernel(per_src, group, dest_ref, probs_ref, grad_ref, gate_up_ref, out_ref, act_ref, row_ref):
    step = pl.program_id(0)
    top, tokens = dest_ref.shape
    lanes = row_ref.shape[2]

    @pl.when(step == 0)
    def _():
        dest = dest_ref[...]
        block_of = ((jnp.maximum(dest, 0) >> 4) * 21846) >> 16
        place = dest - block_of * per_src
        buffer = jnp.where(dest >= 0, block_of >> 5, -1)
        token = lax.broadcasted_iota(jnp.int32, (1, tokens), 1)
        token_parts = [(token >> 1).astype(jnp.float32), (token & 1).astype(jnp.float32)]
        sublanes = lax.broadcasted_iota(jnp.int32, (lanes, tokens), 0)
        places = lax.broadcasted_iota(jnp.int32, (per_src, tokens), 0)
        total = jnp.zeros((5 * per_src, lanes), jnp.float32)
        for k in range(top):
            prob = probs_ref[k : k + 1, :]
            high = prob.astype(jnp.bfloat16).astype(jnp.float32)
            middle = (prob - high).astype(jnp.bfloat16).astype(jnp.float32)
            low = prob - high - middle
            here = places == place[k : k + 1, :]
            values = jnp.concatenate(
                [jnp.where(here, v, 0.0) for v in (*token_parts, high, middle, low)], axis=0
            ).astype(jnp.bfloat16)
            onehot = jnp.where(sublanes == buffer[k : k + 1, :], 1.0, 0.0).astype(jnp.bfloat16)
            total += lax.dot_general(
                values, onehot, (((1,), (1,)), ((), ())), preferred_element_type=jnp.float32
            )
        part = [total[i * per_src : (i + 1) * per_src] for i in range(5)]
        row_ref[0] = 2.0 * part[0] + part[1]
        row_ref[1] = part[2] + part[3] + part[4]

    shift = (lanes - step * group) % lanes
    token_at = pltpu.roll(row_ref[0], shift, 1)
    weight_at = pltpu.roll(row_ref[1], shift, 1)
    columns = lax.broadcasted_iota(jnp.int32, (per_src, tokens), 1).astype(jnp.float32)
    pick = jnp.concatenate(
        [jnp.where(columns == token_at[:, m : m + 1], 1.0, 0.0).astype(jnp.bfloat16) for m in range(group)], axis=0
    )
    weight = jnp.concatenate([weight_at[:, m : m + 1] for m in range(group)], axis=0)
    picked = jnp.dot(pick, grad_ref[...], preferred_element_type=jnp.float32)
    out_ref[...] = (weight * picked).astype(jnp.bfloat16)

    hidden = gate_up_ref.shape[1] // 2
    half = gate_up_ref[:, :hidden].astype(jnp.float32) * 0.5
    up = gate_up_ref[:, hidden:].astype(jnp.float32)
    act_ref[...] = ((half + half * jnp.tanh(half)) * up).astype(jnp.bfloat16).T


def dispatch(out_grad, probs, dest, gate_up, n_ep, per_src):
    tokens, width = out_grad.shape
    top = probs.shape[1]
    slot_rows, hidden2 = gate_up.shape
    group = 8
    steps = 2 * n_ep // group
    block = group * per_src
    return pl.pallas_call(
        functools.partial(dispatch_kernel, per_src, group),
        grid=(steps,),
        in_specs=[
            pl.BlockSpec((top, tokens), lambda i: (0, 0)),
            pl.BlockSpec((top, tokens), lambda i: (0, 0)),
            pl.BlockSpec((tokens, width), lambda i: (0, 0)),
            pl.BlockSpec((block, hidden2), lambda i: (i, 0)),
        ],
        out_specs=[
            pl.BlockSpec((block, width), lambda i: (i, 0)),
            pl.BlockSpec((hidden2 // 2, block), lambda i: (0, i)),
        ],
        out_shape=[
            jax.ShapeDtypeStruct((slot_rows, width), jnp.bfloat16),
            jax.ShapeDtypeStruct((hidden2 // 2, slot_rows), jnp.bfloat16),
        ],
        scratch_shapes=[pltpu.VMEM((2, per_src, 4 * n_ep), jnp.float32)],
        compiler_params=pltpu.CompilerParams(vmem_limit_bytes=VMEM_LIMIT),
    )(dest.T, probs.T, out_grad, gate_up)


def tile_kernel(act_ref, grads_ref, out_ref):
    grads = grads_ref[...].reshape(-1, grads_ref.shape[2])
    tile = jnp.dot(act_ref[...], grads, preferred_element_type=jnp.float32)
    cols = out_ref.shape[2]
    for b in range(out_ref.shape[0]):
        out_ref[b] = tile[:, b * cols : (b + 1) * cols].astype(out_ref.dtype)


def slot_tile(act, grads, slot, n_grp, dtype):
    n_ep, _, per_src, width = grads.shape
    cap = n_ep * per_src
    hidden = act.shape[0]
    cols = width // n_grp
    per_step = 2
    return pl.pallas_call(
        tile_kernel,
        grid=(n_grp // per_step,),
        in_specs=[
            pl.BlockSpec((hidden, cap), lambda i: (0, slot)),
            pl.BlockSpec((n_ep, None, per_src, per_step * cols), lambda i: (0, slot, 0, i)),
        ],
        out_specs=pl.BlockSpec((per_step, hidden, cols), lambda i: (i, 0, 0)),
        out_shape=jax.ShapeDtypeStruct((n_grp, hidden, cols), dtype),
        compiler_params=pltpu.CompilerParams(vmem_limit_bytes=VMEM_LIMIT),
    )(act, grads)


def owner_sum_kernel(owners_ref, pieces_ref, out_ref, sum_ref):
    n_grp, n_ep = owners_ref.shape
    sum_ref[...] = jnp.zeros_like(sum_ref)

    def group(g, carry):
        def one(j, inner):
            owner = owners_ref[g, j]
            sum_ref[owner] += pieces_ref[g * n_ep + j].astype(jnp.float32)
            return inner

        return lax.fori_loop(0, n_ep, one, carry, unroll=8)

    lax.fori_loop(0, n_grp, group, 0)
    out_ref[...] = sum_ref[...].astype(out_ref.dtype)


def owner_sum(owners, pieces, n_ep):
    _, rows, cols = pieces.shape
    return pl.pallas_call(
        owner_sum_kernel,
        in_specs=[
            pl.BlockSpec(memory_space=pltpu.SMEM),
            pl.BlockSpec(memory_space=pltpu.VMEM),
        ],
        out_specs=pl.BlockSpec(memory_space=pltpu.VMEM),
        out_shape=jax.ShapeDtypeStruct((n_ep, rows, cols), jnp.bfloat16),
        scratch_shapes=[pltpu.VMEM((n_ep, rows, cols), jnp.float32)],
        compiler_params=pltpu.CompilerParams(vmem_limit_bytes=VMEM_LIMIT),
    )(owners, pieces)


def on_device(out_grad, probs, dest, replica_owner, gate_up):
    n_ep = lax.axis_size("ep")
    n_grp = lax.axis_size("grp")
    width = out_grad.shape[1]
    cap = gate_up.shape[0] // 2
    hidden = gate_up.shape[1] // 2
    per_src = cap // n_ep
    cols = width // n_grp
    rows = hidden // n_ep

    def exchange(x):
        return lax.all_to_all(x, "ep", split_axis=0, concat_axis=0, tiled=True)

    def share(table, reach):
        return table + lax.ppermute(table, "grp", [(g, g ^ reach) for g in range(n_grp)])

    me = lax.axis_index("grp")
    owners = jnp.where(jnp.arange(n_grp, dtype=jnp.int32)[:, None] == me, replica_owner, 0)
    owners = share(owners, 1)

    outgoing, act = dispatch(out_grad, probs, dest, gate_up, n_ep, per_src)
    outgoing, act, owners = lax.optimization_barrier((outgoing, act, owners))
    incoming = exchange(outgoing.reshape(n_ep, 2 * per_src, width)).reshape(n_ep, 2, per_src, width)
    incoming, owners = lax.optimization_barrier((incoming, owners))

    main_tile = slot_tile(act, incoming, 0, n_grp, jnp.bfloat16)
    owners = share(owners, 2)
    incoming, main_tile, owners = lax.optimization_barrier((incoming, main_tile, owners))

    main_sum = lax.psum_scatter(main_tile, "grp", scatter_dimension=0, tiled=True)
    copy_tile = slot_tile(act, incoming, 1, n_grp, jnp.bfloat16)
    owners = share(owners, 4)
    copy_tile, owners = lax.optimization_barrier((copy_tile, owners))
    pieces = lax.all_to_all(
        copy_tile.reshape(n_grp * n_ep, rows, cols), ("grp", "ep"), split_axis=0, concat_axis=0, tiled=True
    )
    pieces, main_sum = lax.optimization_barrier((pieces, main_sum))
    blocks = owner_sum(owners, pieces, n_ep)
    owned = exchange(blocks).reshape(1, hidden, cols)
    return main_sum.astype(jnp.float32) + owned.astype(jnp.float32)


def solution(mesh):
    in_specs = (
        P(("grp", "ep"), None),
        P(("grp", "ep"), None),
        P(("grp", "ep"), None),
        P("grp", None),
        P(("grp", "ep"), None),
    )
    out_specs = P("ep", None, "grp")
    return jax.shard_map(
        on_device, mesh=mesh, in_specs=in_specs, out_specs=out_specs, check_vma=False
    )
```

```python
import functools

import jax
import jax.numpy as jnp
from jax import lax
from jax.experimental import pallas as pl
from jax.experimental.pallas import tpu as pltpu
from jax.sharding import PartitionSpec as P

VMEM_LIMIT = 20 * 1024 * 1024


def dispatch_kernel(per_src, group, dest_ref, probs_ref, grad_ref, out_ref, row_ref):
    step = pl.program_id(0)
    top, tokens = dest_ref.shape
    lanes = row_ref.shape[2]

    @pl.when(step == 0)
    def _():
        dest = dest_ref[...]
        block_of = ((jnp.maximum(dest, 0) >> 4) * 21846) >> 16
        place = dest - block_of * per_src
        buffer = jnp.where(dest >= 0, block_of >> 5, -1)
        token = lax.broadcasted_iota(jnp.int32, (1, tokens), 1)
        token_parts = [(token >> 1).astype(jnp.float32), (token & 1).astype(jnp.float32)]
        sublanes = lax.broadcasted_iota(jnp.int32, (lanes, tokens), 0)
        places = lax.broadcasted_iota(jnp.int32, (per_src, tokens), 0)
        total = jnp.zeros((5 * per_src, lanes), jnp.float32)
        for k in range(top):
            prob = probs_ref[k : k + 1, :]
            high = prob.astype(jnp.bfloat16).astype(jnp.float32)
            middle = (prob - high).astype(jnp.bfloat16).astype(jnp.float32)
            low = prob - high - middle
            here = places == place[k : k + 1, :]
            values = jnp.concatenate(
                [jnp.where(here, v, 0.0) for v in (*token_parts, high, middle, low)], axis=0
            ).astype(jnp.bfloat16)
            onehot = jnp.where(sublanes == buffer[k : k + 1, :], 1.0, 0.0).astype(jnp.bfloat16)
            total += lax.dot_general(
                values, onehot, (((1,), (1,)), ((), ())), preferred_element_type=jnp.float32
            )
        part = [total[i * per_src : (i + 1) * per_src] for i in range(5)]
        row_ref[0] = 2.0 * part[0] + part[1]
        row_ref[1] = part[2] + part[3] + part[4]

    shift = (lanes - step * group) % lanes
    token_at = pltpu.roll(row_ref[0], shift, 1)
    weight_at = pltpu.roll(row_ref[1], shift, 1)
    columns = lax.broadcasted_iota(jnp.int32, (per_src, tokens), 1).astype(jnp.float32)
    pick = jnp.concatenate(
        [jnp.where(columns == token_at[:, m : m + 1], 1.0, 0.0).astype(jnp.bfloat16) for m in range(group)], axis=0
    )
    weight = jnp.concatenate([weight_at[:, m : m + 1] for m in range(group)], axis=0)
    picked = jnp.dot(pick, grad_ref[...], preferred_element_type=jnp.float32)
    out_ref[...] = (weight * picked).astype(jnp.bfloat16)


def dispatch(out_grad, probs, dest, slot_rows, n_ep, per_src):
    tokens, width = out_grad.shape
    top = probs.shape[1]
    group = 8
    block = group * per_src
    return pl.pallas_call(
        functools.partial(dispatch_kernel, per_src, group),
        grid=(slot_rows // block,),
        in_specs=[
            pl.BlockSpec((top, tokens), lambda i: (0, 0)),
            pl.BlockSpec((top, tokens), lambda i: (0, 0)),
            pl.BlockSpec((tokens, width), lambda i: (0, 0)),
        ],
        out_specs=pl.BlockSpec((block, width), lambda i: (i, 0)),
        out_shape=jax.ShapeDtypeStruct((slot_rows, width), jnp.bfloat16),
        scratch_shapes=[pltpu.VMEM((2, per_src, 4 * n_ep), jnp.float32)],
        compiler_params=pltpu.CompilerParams(vmem_limit_bytes=VMEM_LIMIT),
    )(dest.T, probs.T, out_grad)


def activation_kernel(gate_up_ref, act_ref):
    hidden = gate_up_ref.shape[1] // 2
    half = gate_up_ref[:, :hidden].astype(jnp.float32) * 0.5
    up = gate_up_ref[:, hidden:].astype(jnp.float32)
    act_ref[...] = ((half + half * jnp.tanh(half)) * up).astype(jnp.bfloat16).T


def activations(gate_up):
    slot_rows, hidden2 = gate_up.shape
    block = slot_rows // 8
    return pl.pallas_call(
        activation_kernel,
        grid=(8,),
        in_specs=[pl.BlockSpec((block, hidden2), lambda i: (i, 0))],
        out_specs=pl.BlockSpec((hidden2 // 2, block), lambda i: (0, i)),
        out_shape=jax.ShapeDtypeStruct((hidden2 // 2, slot_rows), jnp.bfloat16),
        compiler_params=pltpu.CompilerParams(vmem_limit_bytes=VMEM_LIMIT),
    )(gate_up)


def tiles_kernel(act_ref, grads_ref, main_ref, copy_ref):
    step = pl.program_id(0)
    half_steps = pl.num_programs(0) // 2
    grads = grads_ref[...].reshape(-1, grads_ref.shape[2])
    tile = jnp.dot(act_ref[...], grads, preferred_element_type=jnp.float32)
    cols = main_ref.shape[2]

    def store(ref):
        for b in range(ref.shape[0]):
            ref[b] = tile[:, b * cols : (b + 1) * cols].astype(ref.dtype)

    @pl.when(step < half_steps)
    def _():
        store(main_ref)

    @pl.when(step >= half_steps)
    def _():
        store(copy_ref)


def slot_tiles(act, grads, n_grp):
    n_ep, _, per_src, width = grads.shape
    cap = n_ep * per_src
    hidden = act.shape[0]
    cols = width // n_grp
    per_step = 2
    half_steps = n_grp // per_step
    return pl.pallas_call(
        tiles_kernel,
        grid=(2 * half_steps,),
        in_specs=[
            pl.BlockSpec((hidden, cap), lambda i: (0, i // half_steps)),
            pl.BlockSpec((n_ep, None, per_src, per_step * cols), lambda i: (0, i // half_steps, 0, i % half_steps)),
        ],
        out_specs=[
            pl.BlockSpec((per_step, hidden, cols), lambda i: (jnp.minimum(i, half_steps - 1), 0, 0)),
            pl.BlockSpec((per_step, hidden, cols), lambda i: (jnp.maximum(i - half_steps, 0), 0, 0)),
        ],
        out_shape=[jax.ShapeDtypeStruct((n_grp, hidden, cols), jnp.bfloat16)] * 2,
        compiler_params=pltpu.CompilerParams(vmem_limit_bytes=VMEM_LIMIT),
    )(act, grads)


def owner_sum_kernel(owners_ref, pieces_ref, out_ref, sum_ref):
    n_grp, n_ep = owners_ref.shape
    sum_ref[...] = jnp.zeros_like(sum_ref)

    def group(g, carry):
        def one(j, inner):
            owner = owners_ref[g, j]
            sum_ref[owner] += pieces_ref[g * n_ep + j].astype(jnp.float32)
            return inner

        return lax.fori_loop(0, n_ep, one, carry, unroll=8)

    lax.fori_loop(0, n_grp, group, 0)
    out_ref[...] = sum_ref[...].astype(out_ref.dtype)


def owner_sum(owners, pieces, n_ep):
    _, rows, cols = pieces.shape
    return pl.pallas_call(
        owner_sum_kernel,
        in_specs=[
            pl.BlockSpec(memory_space=pltpu.SMEM),
            pl.BlockSpec(memory_space=pltpu.VMEM),
        ],
        out_specs=pl.BlockSpec(memory_space=pltpu.VMEM),
        out_shape=jax.ShapeDtypeStruct((n_ep, rows, cols), jnp.bfloat16),
        scratch_shapes=[pltpu.VMEM((n_ep, rows, cols), jnp.float32)],
        compiler_params=pltpu.CompilerParams(vmem_limit_bytes=VMEM_LIMIT),
    )(owners, pieces)


def on_device(out_grad, probs, dest, replica_owner, gate_up):
    n_ep = lax.axis_size("ep")
    n_grp = lax.axis_size("grp")
    width = out_grad.shape[1]
    cap = gate_up.shape[0] // 2
    hidden = gate_up.shape[1] // 2
    per_src = cap // n_ep
    cols = width // n_grp
    rows = hidden // n_ep

    def exchange(x):
        return lax.all_to_all(x, "ep", split_axis=0, concat_axis=0, tiled=True)

    def share(table, reaches):
        return sum(
            (lax.ppermute(table, "grp", [(g, g ^ reach) for g in range(n_grp)]) for reach in reaches), table
        )

    me = lax.axis_index("grp")
    owners = jnp.where(jnp.arange(n_grp, dtype=jnp.int32)[:, None] == me, replica_owner, 0)
    owners = share(owners, [1])

    outgoing = dispatch(out_grad, probs, dest, 2 * cap, n_ep, per_src)
    outgoing, gate_up = lax.optimization_barrier((outgoing, gate_up))
    act = activations(gate_up)
    outgoing, act, owners = lax.optimization_barrier((outgoing, act, owners))
    incoming = exchange(outgoing.reshape(n_ep, 2 * per_src, width)).reshape(n_ep, 2, per_src, width)
    incoming, owners = lax.optimization_barrier((incoming, owners))

    main_tile, copy_tile = slot_tiles(act, incoming, n_grp)
    owners = share(owners, range(2, n_grp, 2))
    main_tile, copy_tile, owners = lax.optimization_barrier((main_tile, copy_tile, owners))

    main_sum = lax.psum_scatter(main_tile, "grp", scatter_dimension=0, tiled=True)
    pieces = lax.all_to_all(
        copy_tile.reshape(n_grp * n_ep, rows, cols), ("grp", "ep"), split_axis=0, concat_axis=0, tiled=True
    )
    pieces, main_sum = lax.optimization_barrier((pieces, main_sum))
    blocks = owner_sum(owners, pieces, n_ep)
    owned = exchange(blocks).reshape(1, hidden, cols)
    return main_sum.astype(jnp.float32) + owned.astype(jnp.float32)


def solution(mesh):
    in_specs = (
        P(("grp", "ep"), None),
        P(("grp", "ep"), None),
        P(("grp", "ep"), None),
        P("grp", None),
        P(("grp", "ep"), None),
    )
    out_specs = P("ep", None, "grp")
    return jax.shard_map(
        on_device, mesh=mesh, in_specs=in_specs, out_specs=out_specs, check_vma=False
    )
```

```python
import functools

import jax
import jax.numpy as jnp
from jax import lax
from jax.experimental import pallas as pl
from jax.experimental.pallas import tpu as pltpu
from jax.sharding import PartitionSpec as P

VMEM_LIMIT = 20 * 1024 * 1024
TILE_VMEM_LIMIT = 56 * 1024 * 1024


def dispatch_kernel(per_src, group, dest_ref, probs_ref, grad_ref, out_ref, row_ref):
    step = pl.program_id(0)
    top, tokens = dest_ref.shape
    lanes = row_ref.shape[2]

    @pl.when(step == 0)
    def _():
        dest = dest_ref[...]
        block_of = ((jnp.maximum(dest, 0) >> 4) * 21846) >> 16
        place = dest - block_of * per_src
        buffer = jnp.where(dest >= 0, block_of >> 5, -1)
        token = lax.broadcasted_iota(jnp.int32, (1, tokens), 1)
        token_parts = [(token >> 1).astype(jnp.float32), (token & 1).astype(jnp.float32)]
        sublanes = lax.broadcasted_iota(jnp.int32, (lanes, tokens), 0)
        places = lax.broadcasted_iota(jnp.int32, (per_src, tokens), 0)
        total = jnp.zeros((5 * per_src, lanes), jnp.float32)
        for k in range(top):
            prob = probs_ref[k : k + 1, :]
            high = prob.astype(jnp.bfloat16).astype(jnp.float32)
            middle = (prob - high).astype(jnp.bfloat16).astype(jnp.float32)
            low = prob - high - middle
            here = places == place[k : k + 1, :]
            values = jnp.concatenate(
                [jnp.where(here, v, 0.0) for v in (*token_parts, high, middle, low)], axis=0
            ).astype(jnp.bfloat16)
            onehot = jnp.where(sublanes == buffer[k : k + 1, :], 1.0, 0.0).astype(jnp.bfloat16)
            total += lax.dot_general(
                values, onehot, (((1,), (1,)), ((), ())), preferred_element_type=jnp.float32
            )
        part = [total[i * per_src : (i + 1) * per_src] for i in range(5)]
        row_ref[0] = 2.0 * part[0] + part[1]
        row_ref[1] = part[2] + part[3] + part[4]

    shift = (lanes - step * group) % lanes
    token_at = pltpu.roll(row_ref[0], shift, 1)
    weight_at = pltpu.roll(row_ref[1], shift, 1)
    columns = lax.broadcasted_iota(jnp.int32, (per_src, tokens), 1).astype(jnp.float32)
    pick = jnp.concatenate(
        [jnp.where(columns == token_at[:, m : m + 1], 1.0, 0.0).astype(jnp.bfloat16) for m in range(group)], axis=0
    )
    weight = jnp.concatenate([weight_at[:, m : m + 1] for m in range(group)], axis=0)
    picked = jnp.dot(pick, grad_ref[...], preferred_element_type=jnp.float32)
    out_ref[...] = (weight * picked).astype(jnp.bfloat16)


def dispatch(out_grad, probs, dest, slot_rows, n_ep, per_src):
    tokens, width = out_grad.shape
    top = probs.shape[1]
    group = 8
    block = group * per_src
    return pl.pallas_call(
        functools.partial(dispatch_kernel, per_src, group),
        grid=(slot_rows // block,),
        in_specs=[
            pl.BlockSpec((top, tokens), lambda i: (0, 0)),
            pl.BlockSpec((top, tokens), lambda i: (0, 0)),
            pl.BlockSpec((tokens, width), lambda i: (0, 0)),
        ],
        out_specs=pl.BlockSpec((block, width), lambda i: (i, 0)),
        out_shape=jax.ShapeDtypeStruct((slot_rows, width), jnp.bfloat16),
        scratch_shapes=[pltpu.VMEM((2, per_src, 4 * n_ep), jnp.float32)],
        compiler_params=pltpu.CompilerParams(vmem_limit_bytes=VMEM_LIMIT),
    )(dest.T, probs.T, out_grad)


def activation_kernel(gate_up_ref, act_ref):
    hidden = gate_up_ref.shape[1] // 2
    half = gate_up_ref[:, :hidden].astype(jnp.float32) * 0.5
    up = gate_up_ref[:, hidden:].astype(jnp.float32)
    act_ref[...] = ((half + half * jnp.tanh(half)) * up).astype(jnp.bfloat16).T


def activations(gate_up):
    slot_rows, hidden2 = gate_up.shape
    block = slot_rows // 8
    return pl.pallas_call(
        activation_kernel,
        grid=(8,),
        in_specs=[pl.BlockSpec((block, hidden2), lambda i: (i, 0))],
        out_specs=pl.BlockSpec((hidden2 // 2, block), lambda i: (0, i)),
        out_shape=jax.ShapeDtypeStruct((hidden2 // 2, slot_rows), jnp.bfloat16),
        compiler_params=pltpu.CompilerParams(vmem_limit_bytes=VMEM_LIMIT),
    )(gate_up)


def tile_kernel(act_ref, grads_ref, out_ref):
    grads = grads_ref[...].reshape(-1, grads_ref.shape[2])
    tile = jnp.dot(act_ref[...], grads, preferred_element_type=jnp.float32)
    cols = out_ref.shape[2]
    for b in range(out_ref.shape[0]):
        out_ref[b] = tile[:, b * cols : (b + 1) * cols].astype(out_ref.dtype)


def slot_tile(act, grads, slot, n_grp, dtype):
    n_ep, _, per_src, width = grads.shape
    cap = n_ep * per_src
    hidden = act.shape[0]
    cols = width // n_grp
    per_step = 2
    return pl.pallas_call(
        tile_kernel,
        grid=(n_grp // per_step,),
        in_specs=[
            pl.BlockSpec((hidden, cap), lambda i: (0, slot)),
            pl.BlockSpec((n_ep, None, per_src, per_step * cols), lambda i: (0, slot, 0, i)),
        ],
        out_specs=pl.BlockSpec((per_step, hidden, cols), lambda i: (i, 0, 0)),
        out_shape=jax.ShapeDtypeStruct((n_grp, hidden, cols), dtype),
        compiler_params=pltpu.CompilerParams(vmem_limit_bytes=TILE_VMEM_LIMIT),
    )(act, grads)


def owner_sum_kernel(owners_ref, pieces_ref, out_ref, sum_ref):
    n_grp, n_ep = owners_ref.shape
    sum_ref[...] = jnp.zeros_like(sum_ref)

    def group(g, carry):
        def one(j, inner):
            owner = owners_ref[g, j]
            sum_ref[owner] += pieces_ref[g * n_ep + j].astype(jnp.float32)
            return inner

        return lax.fori_loop(0, n_ep, one, carry, unroll=8)

    lax.fori_loop(0, n_grp, group, 0)
    out_ref[...] = sum_ref[...].astype(out_ref.dtype)


def owner_sum(owners, pieces, n_ep):
    _, rows, cols = pieces.shape
    return pl.pallas_call(
        owner_sum_kernel,
        in_specs=[
            pl.BlockSpec(memory_space=pltpu.SMEM),
            pl.BlockSpec(memory_space=pltpu.VMEM),
        ],
        out_specs=pl.BlockSpec(memory_space=pltpu.VMEM),
        out_shape=jax.ShapeDtypeStruct((n_ep, rows, cols), jnp.bfloat16),
        scratch_shapes=[pltpu.VMEM((n_ep, rows, cols), jnp.float32)],
        compiler_params=pltpu.CompilerParams(vmem_limit_bytes=VMEM_LIMIT),
    )(owners, pieces)


def on_device(out_grad, probs, dest, replica_owner, gate_up):
    n_ep = lax.axis_size("ep")
    n_grp = lax.axis_size("grp")
    width = out_grad.shape[1]
    cap = gate_up.shape[0] // 2
    hidden = gate_up.shape[1] // 2
    per_src = cap // n_ep
    cols = width // n_grp
    rows = hidden // n_ep

    def exchange(x):
        return lax.all_to_all(x, "ep", split_axis=0, concat_axis=0, tiled=True)

    def share(table, reaches):
        return sum(
            (lax.ppermute(table, "grp", [(g, g ^ reach) for g in range(n_grp)]) for reach in reaches), table
        )

    me = lax.axis_index("grp")
    owners = jnp.where(jnp.arange(n_grp, dtype=jnp.int32)[:, None] == me, replica_owner, 0)
    owners = share(owners, [1])
    outgoing = dispatch(out_grad, probs, dest, 2 * cap, n_ep, per_src)
    outgoing, gate_up, owners = lax.optimization_barrier((outgoing, gate_up, owners))
    owners = share(owners, range(2, n_grp, 2))
    act = activations(gate_up)
    outgoing, act, owners = lax.optimization_barrier((outgoing, act, owners))
    incoming = exchange(outgoing.reshape(n_ep, 2 * per_src, width)).reshape(n_ep, 2, per_src, width)

    main_tile = slot_tile(act, incoming, 0, n_grp, jnp.bfloat16)
    incoming, main_tile = lax.optimization_barrier((incoming, main_tile))
    main_sum = lax.psum_scatter(main_tile, "grp", scatter_dimension=0, tiled=True)
    copy_tile = slot_tile(act, incoming, 1, n_grp, jnp.bfloat16)
    pieces = lax.all_to_all(
        copy_tile.reshape(n_grp * n_ep, rows, cols), ("grp", "ep"), split_axis=0, concat_axis=0, tiled=True
    )
    pieces, main_sum = lax.optimization_barrier((pieces, main_sum))
    blocks = owner_sum(owners, pieces, n_ep)
    owned = exchange(blocks).reshape(1, hidden, cols)
    return main_sum.astype(jnp.float32) + owned.astype(jnp.float32)


def solution(mesh):
    in_specs = (
        P(("grp", "ep"), None),
        P(("grp", "ep"), None),
        P(("grp", "ep"), None),
        P("grp", None),
        P(("grp", "ep"), None),
    )
    out_specs = P("ep", None, "grp")
    return jax.shard_map(
        on_device, mesh=mesh, in_specs=in_specs, out_specs=out_specs, check_vma=False
    )
```

```python
import functools

import jax
import jax.numpy as jnp
from jax import lax
from jax.experimental import pallas as pl
from jax.experimental.pallas import tpu as pltpu
from jax.sharding import PartitionSpec as P

VMEM_LIMIT = 20 * 1024 * 1024
DISPATCH_VMEM_LIMIT = 26 * 1024 * 1024
TILE_VMEM_LIMIT = 46 * 1024 * 1024


def dispatch_kernel(per_src, group, dest_ref, probs_ref, grad_ref, out_ref, row_ref):
    step = pl.program_id(0)
    top, tokens = dest_ref.shape
    lanes = row_ref.shape[2]

    @pl.when(step == 0)
    def _():
        dest = dest_ref[...]
        block_of = ((jnp.maximum(dest, 0) >> 4) * 21846) >> 16
        place = dest - block_of * per_src
        buffer = jnp.where(dest >= 0, block_of >> 5, -1)
        token = lax.broadcasted_iota(jnp.int32, (1, tokens), 1)
        token_parts = [(token >> 1).astype(jnp.float32), (token & 1).astype(jnp.float32)]
        sublanes = lax.broadcasted_iota(jnp.int32, (lanes, tokens), 0)
        places = lax.broadcasted_iota(jnp.int32, (per_src, tokens), 0)
        total = jnp.zeros((5 * per_src, lanes), jnp.float32)
        for k in range(top):
            prob = probs_ref[k : k + 1, :]
            high = prob.astype(jnp.bfloat16).astype(jnp.float32)
            middle = (prob - high).astype(jnp.bfloat16).astype(jnp.float32)
            low = prob - high - middle
            here = places == place[k : k + 1, :]
            values = jnp.concatenate(
                [jnp.where(here, v, 0.0) for v in (*token_parts, high, middle, low)], axis=0
            ).astype(jnp.bfloat16)
            onehot = jnp.where(sublanes == buffer[k : k + 1, :], 1.0, 0.0).astype(jnp.bfloat16)
            total += lax.dot_general(
                values, onehot, (((1,), (1,)), ((), ())), preferred_element_type=jnp.float32
            )
        part = [total[i * per_src : (i + 1) * per_src] for i in range(5)]
        row_ref[0] = 2.0 * part[0] + part[1]
        row_ref[1] = part[2] + part[3] + part[4]

    shift = (lanes - step * group) % lanes
    token_at = pltpu.roll(row_ref[0], shift, 1)
    weight_at = pltpu.roll(row_ref[1], shift, 1)
    columns = lax.broadcasted_iota(jnp.int32, (per_src, tokens), 1).astype(jnp.float32)
    pick = jnp.concatenate(
        [jnp.where(columns == token_at[:, m : m + 1], 1.0, 0.0).astype(jnp.bfloat16) for m in range(group)], axis=0
    )
    weight = jnp.concatenate([weight_at[:, m : m + 1] for m in range(group)], axis=0)
    picked = jnp.dot(pick, grad_ref[...], preferred_element_type=jnp.float32)
    out_ref[...] = (weight * picked).astype(jnp.bfloat16)


def dispatch(out_grad, probs, dest, slot_rows, n_ep, per_src):
    tokens, width = out_grad.shape
    top = probs.shape[1]
    group = 16
    block = group * per_src
    return pl.pallas_call(
        functools.partial(dispatch_kernel, per_src, group),
        grid=(slot_rows // block,),
        in_specs=[
            pl.BlockSpec((top, tokens), lambda i: (0, 0)),
            pl.BlockSpec((top, tokens), lambda i: (0, 0)),
            pl.BlockSpec((tokens, width), lambda i: (0, 0)),
        ],
        out_specs=pl.BlockSpec((block, width), lambda i: (i, 0)),
        out_shape=jax.ShapeDtypeStruct((slot_rows, width), jnp.bfloat16),
        scratch_shapes=[pltpu.VMEM((2, per_src, 4 * n_ep), jnp.float32)],
        compiler_params=pltpu.CompilerParams(vmem_limit_bytes=DISPATCH_VMEM_LIMIT),
    )(dest.T, probs.T, out_grad)


def activation_kernel(gate_up_ref, act_ref):
    hidden = gate_up_ref.shape[1] // 2
    half = gate_up_ref[:, :hidden].astype(jnp.float32) * 0.5
    up = gate_up_ref[:, hidden:].astype(jnp.float32)
    act_ref[...] = ((half + half * jnp.tanh(half)) * up).astype(jnp.bfloat16).T


def activations(gate_up):
    slot_rows, hidden2 = gate_up.shape
    block = slot_rows // 8
    return pl.pallas_call(
        activation_kernel,
        grid=(8,),
        in_specs=[pl.BlockSpec((block, hidden2), lambda i: (i, 0))],
        out_specs=pl.BlockSpec((hidden2 // 2, block), lambda i: (0, i)),
        out_shape=jax.ShapeDtypeStruct((hidden2 // 2, slot_rows), jnp.bfloat16),
        compiler_params=pltpu.CompilerParams(vmem_limit_bytes=VMEM_LIMIT),
    )(gate_up)


def tile_kernel(act_ref, grads_ref, out_ref):
    grads = grads_ref[...].reshape(-1, grads_ref.shape[2])
    tile = jnp.dot(act_ref[...], grads, preferred_element_type=jnp.float32)
    cols = out_ref.shape[2]
    for b in range(out_ref.shape[0]):
        out_ref[b] = tile[:, b * cols : (b + 1) * cols].astype(out_ref.dtype)


def slot_tile(act, grads, slot, n_grp, dtype):
    n_ep, _, per_src, width = grads.shape
    cap = n_ep * per_src
    hidden = act.shape[0]
    cols = width // n_grp
    per_step = 2
    return pl.pallas_call(
        tile_kernel,
        grid=(n_grp // per_step,),
        in_specs=[
            pl.BlockSpec((hidden, cap), lambda i: (0, slot)),
            pl.BlockSpec((n_ep, None, per_src, per_step * cols), lambda i: (0, slot, 0, i)),
        ],
        out_specs=pl.BlockSpec((per_step, hidden, cols), lambda i: (i, 0, 0)),
        out_shape=jax.ShapeDtypeStruct((n_grp, hidden, cols), dtype),
        compiler_params=pltpu.CompilerParams(vmem_limit_bytes=TILE_VMEM_LIMIT),
    )(act, grads)


def owner_sum_kernel(owners_ref, pieces_ref, out_ref, sum_ref):
    n_grp, n_ep = owners_ref.shape
    sum_ref[...] = jnp.zeros_like(sum_ref)

    def group(g, carry):
        def one(j, inner):
            owner = owners_ref[g, j]
            sum_ref[owner] += pieces_ref[g * n_ep + j].astype(jnp.float32)
            return inner

        return lax.fori_loop(0, n_ep, one, carry, unroll=8)

    lax.fori_loop(0, n_grp, group, 0)
    out_ref[...] = sum_ref[...].astype(out_ref.dtype)


def owner_sum(owners, pieces, n_ep):
    _, rows, cols = pieces.shape
    return pl.pallas_call(
        owner_sum_kernel,
        in_specs=[
            pl.BlockSpec(memory_space=pltpu.SMEM),
            pl.BlockSpec(memory_space=pltpu.VMEM),
        ],
        out_specs=pl.BlockSpec(memory_space=pltpu.VMEM),
        out_shape=jax.ShapeDtypeStruct((n_ep, rows, cols), jnp.bfloat16),
        scratch_shapes=[pltpu.VMEM((n_ep, rows, cols), jnp.float32)],
        compiler_params=pltpu.CompilerParams(vmem_limit_bytes=VMEM_LIMIT),
    )(owners, pieces)


def on_device(out_grad, probs, dest, replica_owner, gate_up):
    n_ep = lax.axis_size("ep")
    n_grp = lax.axis_size("grp")
    width = out_grad.shape[1]
    cap = gate_up.shape[0] // 2
    hidden = gate_up.shape[1] // 2
    per_src = cap // n_ep
    cols = width // n_grp
    rows = hidden // n_ep

    def exchange(x):
        return lax.all_to_all(x, "ep", split_axis=0, concat_axis=0, tiled=True)

    def share(table, reaches):
        return sum(
            (lax.ppermute(table, "grp", [(g, g ^ reach) for g in range(n_grp)]) for reach in reaches), table
        )

    me = lax.axis_index("grp")
    owners = jnp.where(jnp.arange(n_grp, dtype=jnp.int32)[:, None] == me, replica_owner, 0)
    owners = share(owners, [1])
    outgoing = dispatch(out_grad, probs, dest, 2 * cap, n_ep, per_src)
    outgoing, gate_up, owners = lax.optimization_barrier((outgoing, gate_up, owners))
    owners = share(owners, range(2, n_grp, 2))
    act = activations(gate_up)
    outgoing, act, owners = lax.optimization_barrier((outgoing, act, owners))
    incoming = exchange(outgoing.reshape(n_ep, 2 * per_src, width)).reshape(n_ep, 2, per_src, width)

    main_tile = slot_tile(act, incoming, 0, n_grp, jnp.bfloat16)
    incoming, main_tile = lax.optimization_barrier((incoming, main_tile))
    main_sum = lax.psum_scatter(main_tile, "grp", scatter_dimension=0, tiled=True)
    copy_tile = slot_tile(act, incoming, 1, n_grp, jnp.bfloat16)
    pieces = lax.all_to_all(
        copy_tile.reshape(n_grp * n_ep, rows, cols), ("grp", "ep"), split_axis=0, concat_axis=0, tiled=True
    )
    pieces, main_sum = lax.optimization_barrier((pieces, main_sum))
    blocks = owner_sum(owners, pieces, n_ep)
    owned = exchange(blocks).reshape(1, hidden, cols)
    return main_sum.astype(jnp.float32) + owned.astype(jnp.float32)


def solution(mesh):
    in_specs = (
        P(("grp", "ep"), None),
        P(("grp", "ep"), None),
        P(("grp", "ep"), None),
        P("grp", None),
        P(("grp", "ep"), None),
    )
    out_specs = P("ep", None, "grp")
    return jax.shard_map(
        on_device, mesh=mesh, in_specs=in_specs, out_specs=out_specs, check_vma=False
    )
```
